32 devices in a mesh: groups: 2 (over y), seq: 4 (over z), head: 2 (over x), sub: 2 (over core).
Axes of the slice: x: 2, y: 2, z: 4, core: 2. Of those that a mesh axis runs over, the one named last changes fastest.
Arguments:
- hidden: bfloat16 [4096, 5376], P(('groups', 'seq'), 'sub'), parts along dimension 0, may hold values from -500 to 500
- norm_gain: float32 [5376], replicated, may hold values from 0.25 to 1.75
- w_query: bfloat16 [5376, 4096], P('seq', ('head', 'sub')), may hold values from -0.078125 to 0.078125
- w_key: bfloat16 [5376, 2048], P('seq', ('head', 'sub')), may hold values from -0.078125 to 0.078125
- w_value: bfloat16 [5376, 2048], P('seq', ('head', 'sub')), may hold values from -0.078125 to 0.078125
- query_gain: float32 [128], replicated, may hold values from 1 to 2.5
- key_gain: float32 [128], replicated, may hold values from 1 to 2.5
- block_source: int32 [32], P('groups'), parts along dimension 0, may hold values from 0 to 15, as said below
- block_doc: int32 [32], P('groups'), parts along dimension 0, may hold values from 0 to 3, never falling along the last dimension, each value on 1 to 8 neighbouring positions
Outputs:
- attention: bfloat16 [4096, 4096], P(('groups', 'seq'), ('head', 'sub')), parts along dimension 0
The draws below stay inside these ranges and needn't reach their ends.
There are 2 independent parts, one for each index of `groups`. The reference program is written for one: setup_inputs(seed, part) draws one part's arguments, and reference() takes and returns one part's arrays. A program takes and returns all parts, laid end to end along the dimension named above; an argument that names none is the same for every part. Nothing has to cross between parts.
Inputs may be any that keep to these rules, and one draw needn't show every extreme that they name: block_source[b] is the arrival slot of block b, rows block_source[b] * 128 to block_source[b] * 128 + 127 of hidden, on shard block_source[b] // 4; each slot holds one block. Block b lies on its own shard b // 4 or on the shard just before or just after it. Of one shard's blocks at most 2 lie on each neighbouring shard, exactly as many as that neighbour's blocks lie on it, and in every draw some shard holds exactly 2 blocks of each of its two neighbours. `block_doc`: document ids never fall along the blocks; each document spans 1 to 8 blocks, one exactly 8.
All inputs are finite; a program needn't handle non-finite values.
Results may differ from the reference program's by a relative error of at most 0.012.
Values may be sent and summed in bfloat16 or wider, within the bound.
A program may use at most 128 MiB of HBM per device.

```python
import math
import jax
import jax.numpy as jnp
import numpy as np
from jax import lax

D = 5376
HEADS = 32
KV_HEADS = 16
HEAD_DIM = 128
WINDOW = 1024
BLOCK = 128
CAP = 2
SHARDS = 4
BPS = 4
NB = 16
TOKENS = 2048
DOCS = 4
MOST_BLOCKS = 8


def draw_hidden(key, part):
    key_noise, key_column, key_row = jax.random.split(key, 3)
    column_scale = jnp.exp(jax.random.uniform(key_column, (1, D), jnp.float32, 0.0, 2.302585))
    row_scale = jnp.exp(jax.random.uniform(key_row, (TOKENS, 1), jnp.float32, 0.0, 2.302585))
    values = jax.random.normal(key_noise, (TOKENS, D), jnp.float32)
    values = jnp.clip(values, -5.0, 5.0)
    return (values * column_scale * row_scale).astype(jnp.bfloat16)


def shard_permutation(sub_key):
    return jax.random.permutation(sub_key, BPS)


def draw_block_source(key, part):
    key_swap, key_spot, key_rank, key_shuffle = jax.random.split(key, 4)
    swaps = jax.random.randint(key_swap, (SHARDS - 1,), 0, CAP + 1).astype(jnp.int32)
    marked = jax.random.randint(key_spot, (), 0, SHARDS - 2)
    pair_ids = jnp.arange(SHARDS - 1)
    swaps = jnp.where((pair_ids == marked) | (pair_ids == marked + 1), CAP, swaps).astype(jnp.int32)
    zero_one = jnp.zeros((1,), jnp.int32)
    to_next = jnp.concatenate([swaps, zero_one])
    to_prior = jnp.concatenate([zero_one, swaps])
    ranking = jax.vmap(shard_permutation)(jax.random.split(key_rank, SHARDS)).astype(jnp.int32)
    shard_ids = jnp.arange(SHARDS, dtype=jnp.int32)[:, None]
    holder = jnp.where(ranking < to_next[:, None], shard_ids + 1, jnp.where(ranking < (to_next + to_prior)[:, None], shard_ids - 1, shard_ids)).reshape(NB)
    block_ids = jnp.arange(NB, dtype=jnp.int32)
    earlier = (holder[None, :] == holder[:, None]) & (block_ids[None, :] < block_ids[:, None])
    order_in = jnp.sum(earlier.astype(jnp.int32), axis=1)
    shuffle = jax.vmap(shard_permutation)(jax.random.split(key_shuffle, SHARDS)).astype(jnp.int32)
    return (holder * BPS + shuffle[holder, order_in]).astype(jnp.int32)


def levels(stream_key, shape, cuts, least, top_value):
    level, own = 1.0, jax.random.fold_in(stream_key, 6)
    for axis_at, blocks in cuts:
        heights = jnp.exp(jax.random.uniform(jax.random.fold_in(own, axis_at), (blocks,), jnp.float32, least / len(cuts), top_value / len(cuts)))
        level = level * jnp.repeat(heights, shape[axis_at] // blocks).reshape([-1 if axis == axis_at else 1 for axis in range(len(shape))])
    return level


def profile(count, total, reach, lean):
    loads = [(1 << 20) // math.isqrt(rank ** lean) + 1 for rank in range(2, count + 1)]
    spare, counts = total - reach - (count - 1), [1] * (count - 1)
    while spare > 0:
        free = [i for i in range(count - 1) if counts[i] < reach]
        pool, remaining = sum([loads[i] for i in free]), spare
        for i in free:
            addition = min(reach - counts[i], max(1, remaining * loads[i] // pool), spare)
            counts[i] = counts[i] + addition
            spare = spare - addition
    return np.array([reach] + counts)


def ragged_sizes(key, count, total, limit, slope):
    if count == 2:
        one = jax.random.randint(key, (), max(1, total - limit), min(limit, total - 1) + 1)
        return jnp.stack([one, total - one])
    sizes = jnp.asarray(profile(count, total, limit, slope), jnp.int32)
    pairs = (count - 1) // 2
    donor, sink = sizes[1:1 + 2 * pairs:2], sizes[2:2 + 2 * pairs:2]
    room = jnp.minimum(donor - 1, limit - sink)
    moved = jax.random.randint(jax.random.fold_in(key, 1), (pairs,), 0, 1 << 20) % (room + 1)
    sizes = sizes.at[1:1 + 2 * pairs:2].set(donor - moved).at[2:2 + 2 * pairs:2].set(sink + moved)
    return sizes[jax.random.permutation(jax.random.fold_in(key, 2), count)]


def gaussian(stream_key, extent, spread, limit, cuts=(), kind=jnp.bfloat16):
    values = jax.random.normal(stream_key, extent, jnp.float32) * spread
    if len(cuts) > 0:
        values = levels(stream_key, extent, cuts, -0.22, 0.18) * values
    return jnp.clip(values, min=-limit, max=limit).astype(kind)


def setup_inputs(seed: int = 0, part: int = 0) -> dict:
    arg_keys = jax.random.split(jax.random.key(seed), 10)
    part_splits = jax.random.split(jax.random.fold_in(arg_keys[9], part), 10)
    return {
        "hidden": draw_hidden(jax.random.fold_in(jax.random.fold_in(arg_keys[9], part), 71), part),
        "norm_gain": jnp.clip(1.0 + 0.15 * jax.random.normal(arg_keys[1], (D,), jnp.float32), 0.25, 1.75),
        "w_query": gaussian(arg_keys[2], (D, HEADS * HEAD_DIM), D ** -0.5, 0.078125, ((0, 4), (1, 4))),
        "w_key": gaussian(arg_keys[3], (D, KV_HEADS * HEAD_DIM), D ** -0.5, 0.078125, ((0, 4), (1, 4))),
        "w_value": gaussian(arg_keys[4], (D, KV_HEADS * HEAD_DIM), D ** -0.5, 0.078125, ((0, 4), (1, 4))),
        "query_gain": jnp.clip(jnp.exp(jax.random.uniform(arg_keys[5], (HEAD_DIM,), jnp.float32, math.log(1.0), math.log(2.5))), 1.0, 2.5),
        "key_gain": jnp.clip(jnp.exp(jax.random.uniform(arg_keys[6], (HEAD_DIM,), jnp.float32, math.log(1.0), math.log(2.5))), 1.0, 2.5),
        "block_source": draw_block_source(jax.random.fold_in(jax.random.fold_in(arg_keys[9], part), 71), part),
        "block_doc": jnp.searchsorted(jnp.cumsum(ragged_sizes(part_splits[8], DOCS, NB, MOST_BLOCKS, 2)), jnp.arange(NB), side="right").astype(jnp.int32),
    }


QUERY_SCALE = 168.0 ** (-0.5)
EPSILON = 1e-06
ROPE_BASE = 10000.0

def table_lookup(table, indices):
    hits = indices[:, None] == jnp.arange(table.shape[0], dtype=jnp.int32)[None, :]
    return lax.optimization_barrier(jnp.sum(jnp.where(hits, table[None, :], 0), axis=1)).astype(jnp.int32)

def token_positions(block_ids, block_doc):
    first_block = lax.optimization_barrier(jnp.sum((block_doc[None, :] < block_doc[:, None]).astype(jnp.int32), axis=1))
    start_block = table_lookup(first_block, block_ids)
    within = jnp.arange(BLOCK, dtype=jnp.int32)
    return ((block_ids - start_block)[:, None] * BLOCK + within[None, :]).reshape(-1).astype(jnp.float32)

def token_docs(token_ids, block_doc):
    return table_lookup(block_doc, jnp.floor_divide(token_ids, BLOCK).astype(jnp.int32))

def head_rotation(values, gain, positions, factor):
    token_count = values.shape[0]
    per_head = values.reshape(token_count, -1, HEAD_DIM)
    normed = per_head * lax.rsqrt(lax.optimization_barrier(jnp.mean(per_head * per_head, axis=2, keepdims=True)) + EPSILON) * gain
    half_dim = HEAD_DIM // 2
    frequency = ROPE_BASE ** (-(jnp.arange(half_dim, dtype=jnp.float32) * 2.0 / HEAD_DIM))
    angles = positions[:, None] * frequency[None, :]
    cosine = jnp.cos(angles)[:, None, :]
    sine_table = jnp.sin(angles)[:, None, :]
    first_half = normed[:, :, :half_dim]
    second_half = normed[:, :, half_dim:]
    turned = jnp.concatenate([first_half * cosine - second_half * sine_table, second_half * cosine + first_half * sine_table], axis=2)
    return (turned * factor).reshape(token_count, -1).astype(jnp.bfloat16)

def attend_block(query_rows, key_rows, value_rows, query_tokens, key_tokens, query_docs, key_docs):
    query_count = query_rows.shape[0]
    key_count = key_rows.shape[0]
    kv_count = key_rows.shape[1] // HEAD_DIM
    query_heads = lax.optimization_barrier(query_rows).astype(jnp.float32).reshape(query_count, kv_count, 2, HEAD_DIM)
    key_heads = lax.optimization_barrier(key_rows).astype(jnp.float32).reshape(key_count, kv_count, HEAD_DIM)
    value_heads = lax.optimization_barrier(value_rows).astype(jnp.float32).reshape(key_count, kv_count, HEAD_DIM)
    scores = jnp.einsum('qgjd,kgd->gjqk', query_heads, key_heads)
    allowed = (key_tokens[None, :] >= 0) & (key_tokens[None, :] <= query_tokens[:, None])
    allowed = allowed & (query_tokens[:, None] - key_tokens[None, :] < WINDOW) & (key_docs[None, :] == query_docs[:, None])
    weight_exp = jnp.where(allowed, jnp.exp(scores), 0.0)
    totals = lax.optimization_barrier(jnp.sum(weight_exp, axis=3))
    weight_low = lax.optimization_barrier(weight_exp.astype(jnp.bfloat16)).astype(jnp.float32)
    summed = jnp.einsum('gjqk,kgd->qgjd', weight_low, value_heads)
    return (summed / jnp.transpose(totals, (2, 0, 1))[:, :, :, None]).reshape(query_count, -1).astype(jnp.bfloat16)

def reference(hidden, norm_gain, w_query, w_key, w_value, query_gain, key_gain, block_source, block_doc):
    block_total = block_source.shape[0]
    ordered = hidden.reshape(block_total, BLOCK, -1)[block_source].reshape(TOKENS, -1)
    as_float = ordered.astype(jnp.float32)
    normed = (as_float * lax.rsqrt(lax.optimization_barrier(jnp.mean(as_float * as_float, axis=1, keepdims=True)) + EPSILON) * norm_gain).astype(jnp.bfloat16)
    query_raw = jnp.dot(normed, w_query, preferred_element_type=jnp.float32)
    key_raw = jnp.dot(normed, w_key, preferred_element_type=jnp.float32)
    value_low = jnp.dot(normed, w_value, preferred_element_type=jnp.float32).astype(jnp.bfloat16)
    positions = token_positions(jnp.arange(block_total, dtype=jnp.int32), block_doc)
    query_rot = head_rotation(query_raw, query_gain, positions, QUERY_SCALE)
    key_rot = head_rotation(key_raw, key_gain, positions, 1.0)
    key_padded = jnp.concatenate([jnp.zeros((WINDOW, key_rot.shape[1]), jnp.bfloat16), key_rot], axis=0)
    value_padded = jnp.concatenate([jnp.zeros((WINDOW, value_low.shape[1]), jnp.bfloat16), value_low], axis=0)
    block_rows = min(512, TOKENS)

    def one_block(block_index):
        first_row = block_index * block_rows
        query_tokens = first_row + jnp.arange(block_rows, dtype=jnp.int32)
        key_tokens = first_row - WINDOW + jnp.arange(block_rows + WINDOW, dtype=jnp.int32)
        return attend_block(lax.dynamic_slice_in_dim(query_rot, first_row, block_rows, 0), lax.dynamic_slice_in_dim(key_padded, first_row, block_rows + WINDOW, 0), lax.dynamic_slice_in_dim(value_padded, first_row, block_rows + WINDOW, 0), query_tokens, key_tokens, token_docs(query_tokens, block_doc), token_docs(key_tokens, block_doc))
    result = lax.map(one_block, jnp.arange(TOKENS // block_rows, dtype=jnp.int32))
    return result.reshape(TOKENS, -1)
```

```python
import functools

import jax
import jax.numpy as jnp
from jax import lax
from jax.experimental import pallas as pl
from jax.experimental.pallas import tpu as pltpu
from jax.sharding import PartitionSpec as P

HEAD_DIM = 128
WINDOW = 1024
BLOCK = 128
CAP = 2


QUERY_SCALE = 168.0 ** (-0.5)
EPSILON = 1e-06
ROPE_BASE = 10000.0


def passed_along(x, axis, by):
    size = lax.axis_size(axis)
    pairs = [(i, i + by) for i in range(size) if 0 <= i + by < size]
    return lax.ppermute(x, axis, pairs)


def table_lookup(table, indices):
    hits = indices[:, None] == jnp.arange(table.shape[0], dtype=jnp.int32)[None, :]
    return jnp.sum(jnp.where(hits, table[None, :], 0), axis=1)


def token_positions(block_ids, block_doc):
    first_block = jnp.sum((block_doc[None, :] < block_doc[:, None]).astype(jnp.int32), axis=1)
    start_block = table_lookup(first_block, block_ids)
    within = jnp.arange(BLOCK, dtype=jnp.int32)
    return (
        ((block_ids - start_block)[:, None] * BLOCK + within[None, :])
        .reshape(-1)
        .astype(jnp.float32)
    )


def token_docs(token_ids, block_doc):
    return table_lookup(block_doc, jnp.floor_divide(token_ids, BLOCK))


def head_rotation(values, gain, positions, factor):
    token_count = values.shape[0]
    per_head = values.reshape(token_count, -1, HEAD_DIM)
    normed = (
        per_head * lax.rsqrt(jnp.mean(per_head * per_head, axis=2, keepdims=True) + EPSILON) * gain
    )
    half_dim = HEAD_DIM // 2
    frequency = ROPE_BASE ** (-(jnp.arange(half_dim, dtype=jnp.float32) * 2.0 / HEAD_DIM))
    angles = positions[:, None] * frequency[None, :]
    cosine = jnp.cos(angles)[:, None, :]
    sine_table = jnp.sin(angles)[:, None, :]
    first_half = normed[:, :, :half_dim]
    second_half = normed[:, :, half_dim:]
    turned = jnp.concatenate(
        [
            first_half * cosine - second_half * sine_table,
            second_half * cosine + first_half * sine_table,
        ],
        axis=2,
    )
    return (turned * factor).reshape(token_count, -1).astype(jnp.bfloat16)


def side_ranks(labels):
    length = labels.shape[0]
    earlier = jnp.arange(length)[None, :] < jnp.arange(length)[:, None]
    matching = labels[None, :] == labels[:, None]
    return jnp.sum((earlier & matching).astype(jnp.int32), axis=1)


def outgoing_slots(block_source, target, own_shard, block_count, shard_count):
    first_slot = jnp.clip(target, 0, shard_count - 1) * block_count
    slot_ids = lax.dynamic_slice_in_dim(block_source, first_slot, block_count)
    sending = (slot_ids // block_count == own_shard) & (target >= 0) & (target < shard_count)
    send_rank = side_ranks(sending.astype(jnp.int32))
    wanted = (jnp.arange(CAP)[:, None] == send_rank[None, :]) & sending[None, :]
    return jnp.sum(jnp.where(wanted, (slot_ids % block_count)[None, :], 0), axis=1)


def incoming_index(block_source, own_shard, block_count):
    slot_ids = lax.dynamic_slice_in_dim(block_source, own_shard * block_count, block_count)
    sides = slot_ids // block_count - own_shard
    side_rank = side_ranks(sides)
    from_prior = block_count + side_rank
    from_next = block_count + CAP + side_rank
    return jnp.where(
        sides == 0, slot_ids % block_count, jnp.where(sides < 0, from_prior, from_next)
    )


def blocks_at(pieces, chosen):
    picked = [
        lax.dynamic_slice_in_dim(pieces, chosen[i], 1, 0) for i in range(chosen.shape[0])
    ]
    return jnp.concatenate(picked, axis=0)


def migrate(values, block_source, own_shard, shard_count):
    row_count, col_count = values.shape
    block_count = row_count // BLOCK
    pieces = values.reshape(block_count, BLOCK, col_count)
    block_pool = [pieces]
    for offset in (1, -1):
        chosen = outgoing_slots(
            block_source, own_shard + offset, own_shard, block_count, shard_count
        )
        outgoing = blocks_at(pieces, chosen)
        block_pool.append(passed_along(outgoing, "seq", offset))
    joined = jnp.concatenate(block_pool, axis=0)
    placed = blocks_at(joined, incoming_index(block_source, own_shard, block_count))
    return placed.reshape(row_count, col_count)


def gathered(x, axis, dim):
    size = lax.axis_size(axis)
    index = lax.axis_index(axis)
    extent = x.shape[dim]
    shape = list(x.shape)
    shape[dim] = extent * size
    whole = jnp.zeros(shape, x.dtype)
    pairs = [(i, (i + 1) % size) for i in range(size)]
    for step in range(size):
        owner = lax.rem(index + size - step, size)
        whole = lax.dynamic_update_slice_in_dim(whole, x, owner * extent, dim)
        if step < size - 1:
            x = lax.ppermute(x, axis, pairs)
    return whole


def project_rows(halves, norm_gain, w_query, w_key, w_value, query_gain, key_gain, positions):
    full_rows = gathered(halves, "sub", 1)
    as_float = full_rows.astype(jnp.float32)
    normed = (
        as_float
        * lax.rsqrt(jnp.mean(as_float * as_float, axis=1, keepdims=True) + EPSILON)
        * norm_gain
    ).astype(jnp.bfloat16)
    segments = (
        gathered(w_query, "seq", 0),
        gathered(w_key, "seq", 0),
        gathered(w_value, "seq", 0),
    )
    query_raw, key_raw, value_raw = tuple(
        (jnp.dot(normed, segment, preferred_element_type=jnp.float32) for segment in segments)
    )
    query_rot = head_rotation(query_raw, query_gain, positions, QUERY_SCALE)
    key_rot = head_rotation(key_raw, key_gain, positions, 1.0)
    return jnp.concatenate([query_rot, key_rot, value_raw.astype(jnp.bfloat16)], axis=1)


def attend_block(query_rows, key_rows, value_rows, query_tokens, key_tokens, query_docs, key_docs):
    query_count = query_rows.shape[0]
    key_count = key_rows.shape[0]
    kv_count = key_rows.shape[1] // HEAD_DIM
    query_heads = query_rows.reshape(query_count, kv_count, 2, HEAD_DIM)
    key_heads = key_rows.reshape(key_count, kv_count, HEAD_DIM)
    value_heads = value_rows.reshape(key_count, kv_count, HEAD_DIM)
    scores = jnp.einsum(
        "qgjd,kgd->gjqk", query_heads, key_heads, preferred_element_type=jnp.float32
    )
    allowed = (key_tokens[None, :] >= 0) & (key_tokens[None, :] <= query_tokens[:, None])
    allowed = (
        allowed
        & (query_tokens[:, None] - key_tokens[None, :] < WINDOW)
        & (key_docs[None, :] == query_docs[:, None])
    )
    weight_exp = jnp.where(allowed, jnp.exp(scores), 0.0)
    totals = jnp.sum(weight_exp, axis=3)
    summed = jnp.einsum(
        "gjqk,kgd->qgjd",
        weight_exp.astype(jnp.bfloat16),
        value_heads,
        preferred_element_type=jnp.float32,
    )
    return (
        (summed / jnp.transpose(totals, (2, 0, 1))[:, :, :, None])
        .reshape(query_count, -1)
        .astype(jnp.bfloat16)
    )


def body(hidden, norm_gain, w_query, w_key, w_value, query_gain, key_gain, block_source, block_doc):
    row_count = hidden.shape[0]
    block_count = row_count // BLOCK
    own_shard = lax.axis_index("seq")
    shard_count = lax.axis_size("seq")
    own_blocks = own_shard * block_count + jnp.arange(block_count, dtype=jnp.int32)
    moved = migrate(hidden, block_source, own_shard, shard_count)
    packed = project_rows(
        moved,
        norm_gain,
        w_query,
        w_key,
        w_value,
        query_gain,
        key_gain,
        token_positions(own_blocks, block_doc),
    )
    query_width = w_query.shape[1]
    key_width = w_key.shape[1]
    query_rot = packed[:, :query_width]
    key_value = packed[:, query_width:]
    halo_count = max(1, WINDOW // row_count)
    received = []
    for distance in range(halo_count, 0, -1):
        received.append(passed_along(key_value, "seq", distance))
    extended = jnp.concatenate(received + [key_value], axis=0)
    key_all = extended[:, :key_width]
    value_all = extended[:, key_width:]
    query_tokens = own_shard * row_count + jnp.arange(row_count, dtype=jnp.int32)
    key_tokens = own_shard * row_count - WINDOW + jnp.arange(extended.shape[0], dtype=jnp.int32)
    query_docs = token_docs(query_tokens, block_doc)
    key_docs = token_docs(key_tokens, block_doc)
    block_rows = min(512, row_count)

    def one_block(block_index):
        return attend_block(
            query_rot, key_all, value_all, query_tokens, key_tokens, query_docs, key_docs
        )

    result = lax.map(one_block, jnp.arange(row_count // block_rows, dtype=jnp.int32))
    return result.reshape(row_count, -1)


MESH = pl.DeviceIdType.MESH
CHUNKS = 4
VMEM_LIMIT = 48 * 1024 * 1024


def remote(src, dst, send_sem, recv_sem, **target):
    return pltpu.make_async_remote_copy(
        src_ref=src,
        dst_ref=dst,
        send_sem=send_sem,
        recv_sem=recv_sem,
        device_id=target,
        device_id_type=MESH,
    )


def gather_kernel(
    shards, own_rows, wq, wk, wv, rows, weights,
    zr_send, zr_recv, zl_send, zl_recv, x_send, x_recv, c_send, c_recv,
    w_send, w_recv, y_send, y_recv, own_sem, ownw_sem,
):
    y, z = lax.axis_index("groups"), lax.axis_index("seq")
    x, c = lax.axis_index("head"), lax.axis_index("sub")
    chunks = own_rows.shape[1]
    widths = (wq.shape[2] // shards, wk.shape[2] // shards, wv.shape[2] // shards)
    starts = (0, widths[0], widths[0] + widths[1])

    barrier = pltpu.get_barrier_semaphore()
    for d in range(1, shards):
        pl.semaphore_signal(
            barrier, inc=1, device_id={"seq": lax.rem(z + d, shards)}, device_id_type=MESH
        )
    pl.semaphore_signal(barrier, inc=1, device_id={"groups": 1 - y}, device_id_type=MESH)
    pl.semaphore_signal(barrier, inc=1, device_id={"head": 1 - x}, device_id_type=MESH)
    pl.semaphore_signal(barrier, inc=1, device_id={"sub": 1 - c}, device_id_type=MESH)
    pl.semaphore_wait(barrier, shards + 2)

    def along(step, j, right):
        s = z - step if right else z + step
        src = own_rows.at[x, j] if step == 0 else rows.at[s, c, x, j]
        send, recv = (zr_send, zr_recv) if right else (zl_send, zl_recv)
        return remote(
            src, rows.at[s, c, x, j], send.at[step, j], recv.at[step + 1, j],
            seq=z + 1 if right else z - 1,
        )

    def along_recv(step, j, right):
        s = z - step if right else z + step
        send, recv = (zr_send, zr_recv) if right else (zl_send, zl_recv)
        return remote(
            rows.at[s, c, x, j], rows.at[s, c, x, j], send.at[0, j], recv.at[step, j],
            seq=z - 1 if right else z + 1,
        )

    def across(s, j, half):
        return remote(
            rows.at[s, c, half, j], rows.at[s, c, half, j], x_send.at[s, j], x_recv.at[s, j],
            head=1 - x,
        )

    def to_core(s, half, j, own=False):
        src = own_rows.at[half, j] if own else rows.at[s, c, half, j]
        return remote(
            src, rows.at[s, c, half, j], c_send.at[s, half, j], c_recv.at[s, half, j], sub=1 - c
        )

    def from_core(s, half, j):
        where = rows.at[s, 1 - c, half, j]
        return remote(where, where, c_send.at[s, half, j], c_recv.at[s, half, j], sub=1 - c)

    def weight_piece(d, n):
        t = lax.rem(z + d, shards)
        src = (wq, wk, wv)[n].at[y, :, pl.ds(pl.multiple_of(t * widths[n], widths[n]), widths[n])]
        return remote(
            src, weights.at[z, y, :, pl.ds(starts[n], widths[n])],
            w_send.at[d, n], w_recv.at[d, n], seq=t,
        )

    def weight_arrival(d, n):
        s = lax.rem(z + shards - d, shards)
        where = weights.at[s, y, :, pl.ds(starts[n], widths[n])]
        return remote(where, where, w_send.at[d, n], w_recv.at[d, n], seq=s)

    def weight_across(d, half):
        s = lax.rem(z + shards - d, shards)
        where = weights.at[s, half]
        return remote(where, where, y_send.at[d], y_recv.at[d], groups=1 - y)

    def own_weight(n):
        src = (wq, wk, wv)[n].at[:, :, pl.ds(pl.multiple_of(z * widths[n], widths[n]), widths[n])]
        return pltpu.make_async_copy(
            src, weights.at[z, :, :, pl.ds(starts[n], widths[n])], ownw_sem.at[n]
        )

    def own_copy():
        return pltpu.make_async_copy(own_rows, rows.at[z, c], own_sem)

    for j in range(chunks):
        for right in (True, False):

            @pl.when(z + 1 < shards if right else z > 0)
            def _():
                along(0, j, right).start()

    for d in range(1, shards):
        for n in range(3):
            weight_piece(d, n).start()
    for j in range(chunks):
        to_core(z, 0, j, True).start()
        to_core(z, 1, j, True).start()
    own_copy().start()
    for n in range(3):
        own_weight(n).start()

    def has(step, right):
        return z - step >= 0 if right else z + step < shards

    def second_hop(step, j):
        for right in (True, False):

            @pl.when(has(step, right))
            def _():
                s = z - step if right else z + step
                across(s, j, 1 - x).wait_recv()
                to_core(s, 1 - x, j).start()

    order = [(step, j) for step in range(1, shards) for j in range(chunks)]
    for i, (step, j) in enumerate(order):
        for right in (True, False):

            @pl.when(has(step, right))
            def _():
                s = z - step if right else z + step
                along_recv(step, j, right).wait_recv()

                @pl.when(z + 1 < shards if right else z > 0)
                def _():
                    along(step, j, right).start()

                across(s, j, x).start()
                to_core(s, x, j).start()

        if j == chunks - 1:
            for n in range(3):
                weight_arrival(step, n).wait_recv()
            weight_across(step, y).start()
        if i > 0:
            second_hop(*order[i - 1])
    second_hop(*order[-1])

    for d in range(1, shards):
        weight_across(d, 1 - y).wait_recv()
    for s in range(shards):
        for half in range(2):
            for j in range(chunks):
                from_core(s, half, j).wait_recv()
    own_copy().wait()
    for n in range(3):
        own_weight(n).wait()
    for d in range(1, shards):
        for n in range(3):
            weight_piece(d, n).wait_send()
        weight_across(d, y).wait_send()
    for step in range(shards):
        for right in (True, False):

            @pl.when(has(step, right) & (z + 1 < shards if right else z > 0))
            def _():
                for j in range(chunks):
                    along(step, j, right).wait_send()

            if step > 0:

                @pl.when(has(step, right))
                def _():
                    s = z - step if right else z + step
                    for j in range(chunks):
                        across(s, j, x).wait_send()
    for s in range(shards):
        for half in range(2):
            for j in range(chunks):
                to_core(s, half, j).wait_send()


def gather_all(normed, w_query, w_key, w_value, shards):
    row_count, width = normed.shape
    depth = w_query.shape[0]
    chunk = row_count // (2 * CHUNKS)
    total = (w_query.shape[1] + w_key.shape[1] + w_value.shape[1]) // shards
    halves = [w.reshape(2, depth // 2, w.shape[1]) for w in (w_query, w_key, w_value)]
    dma = pltpu.SemaphoreType.DMA
    line = dma((shards + 1, CHUNKS))
    anywhere = pl.BlockSpec(memory_space=pl.ANY)
    return pl.pallas_call(
        functools.partial(gather_kernel, shards),
        out_shape=(
            jax.ShapeDtypeStruct((shards, 2, 2, CHUNKS, chunk, width), jnp.bfloat16),
            jax.ShapeDtypeStruct((shards, 2, depth // 2, total), jnp.bfloat16),
        ),
        in_specs=[anywhere] * 4,
        out_specs=(anywhere, anywhere),
        scratch_shapes=[
            line, line, line, line, line, line,
            dma((shards, 2, CHUNKS)), dma((shards, 2, CHUNKS)),
            dma((shards, 3)), dma((shards, 3)), dma((shards,)), dma((shards,)),
            dma, dma((3,)),
        ],
        compiler_params=pltpu.CompilerParams(collective_id=0, has_side_effects=True),
        name="gather_all",
    )(normed.reshape(2, CHUNKS, chunk, width), *halves)


def project_kernel(count, source, *refs):
    xs = refs[:count]
    weights, gains, cosine, sine, q_out, k_out, v_out = refs[count:]
    width = xs[0].shape[-1]
    low = jnp.concatenate([r[0, 0, 0] for r in xs], axis=0)
    high = jnp.concatenate([r[0, 1, 0] for r in xs], axis=0)
    acc = jnp.dot(low, weights[:width], preferred_element_type=jnp.float32)
    acc = acc + jnp.dot(high, weights[width:], preferred_element_type=jnp.float32)

    def turned(u, gain, factor):
        n = u * lax.rsqrt(jnp.mean(u * u, axis=1, keepdims=True) + EPSILON) * gain
        swapped = pltpu.roll(n, HEAD_DIM // 2, 1)
        return ((n * cosine[...] + swapped * sine[...]) * factor).astype(jnp.bfloat16)

    for h in range(2):
        cols = slice(h * HEAD_DIM, (h + 1) * HEAD_DIM)
        q_out[:, cols] = turned(acc[:, cols], gains[0:1, :], QUERY_SCALE)
    k_out[...] = turned(acc[:, 2 * HEAD_DIM : 3 * HEAD_DIM], gains[1:2, :], 1.0)
    v_out[...] = acc[:, 3 * HEAD_DIM :].astype(jnp.bfloat16)


def project_all(rows, weights, gains, cosine, sine, block_source, per_shard):
    count = 2
    blocks = block_source.shape[0]
    width = rows.shape[-1]
    tokens = blocks * BLOCK
    step = count * BLOCK

    def picked(n):
        def index(i, source):
            slot = source[count * i + n]
            return (slot // per_shard, 0, slot % per_shard, 0, 0)

        return pl.BlockSpec((1, 2, 1, BLOCK, width), index)

    return pl.pallas_call(
        functools.partial(project_kernel, count),
        grid_spec=pltpu.PrefetchScalarGridSpec(
            num_scalar_prefetch=1,
            grid=(blocks // count,),
            in_specs=[picked(n) for n in range(count)]
            + [
                pl.BlockSpec(weights.shape, lambda i, source: (0, 0)),
                pl.BlockSpec(gains.shape, lambda i, source: (0, 0)),
                pl.BlockSpec((step, HEAD_DIM), lambda i, source: (i, 0)),
                pl.BlockSpec((step, HEAD_DIM), lambda i, source: (i, 0)),
            ],
            out_specs=[
                pl.BlockSpec((step, 2 * HEAD_DIM), lambda i, source: (i, 0)),
                pl.BlockSpec((step, HEAD_DIM), lambda i, source: (i, 0)),
                pl.BlockSpec((step, HEAD_DIM), lambda i, source: (i, 0)),
            ],
        ),
        out_shape=(
            jax.ShapeDtypeStruct((tokens, 2 * HEAD_DIM), jnp.bfloat16),
            jax.ShapeDtypeStruct((tokens, HEAD_DIM), jnp.bfloat16),
            jax.ShapeDtypeStruct((tokens, HEAD_DIM), jnp.bfloat16),
        ),
        compiler_params=pltpu.CompilerParams(vmem_limit_bytes=VMEM_LIMIT),
        name="project_all",
    )(block_source, *([rows] * count), weights, gains, cosine, sine)


def attend_kernel(first, q_ref, k_ref, v_ref, out_ref):
    b = pl.program_id(0)
    span = 2 * BLOCK
    query = jnp.concatenate([q_ref[:, :HEAD_DIM], q_ref[:, HEAD_DIM:]], axis=0)
    start = first[b] * BLOCK
    lowest = jnp.maximum(first[b], b - WINDOW // BLOCK)
    token = b * BLOCK + lax.rem(lax.broadcasted_iota(jnp.int32, (span, span), 0), BLOCK)
    lane = lax.broadcasted_iota(jnp.int32, (span, span), 1)
    least = jnp.maximum(start, token - (WINDOW - 1))

    def step(i, carry):
        acc, total = carry
        at = pl.multiple_of(i * span, span)
        keys = k_ref[pl.ds(at, span), :]
        scores = lax.dot_general(
            query, keys, (((1,), (1,)), ((), ())), preferred_element_type=jnp.float32
        )
        other = lane + at
        allowed = (other <= token) & (other >= least)
        weight = jnp.where(allowed, jnp.exp(scores), 0.0)
        total = total + weight[:, :HEAD_DIM] + weight[:, HEAD_DIM:]
        acc = acc + jnp.dot(
            weight.astype(jnp.bfloat16),
            v_ref[pl.ds(at, span), :],
            preferred_element_type=jnp.float32,
        )
        return acc, total

    zero = jnp.zeros((span, HEAD_DIM), jnp.float32)
    acc, total = lax.fori_loop(lowest // 2, b // 2 + 1, step, (zero, zero))
    result = (acc / jnp.sum(total, axis=1, keepdims=True)).astype(jnp.bfloat16)
    out_ref[:, :HEAD_DIM] = result[:BLOCK]
    out_ref[:, HEAD_DIM:] = result[BLOCK:]


def attend_all(query, key, value, first):
    tokens = query.shape[0]
    return pl.pallas_call(
        attend_kernel,
        grid_spec=pltpu.PrefetchScalarGridSpec(
            num_scalar_prefetch=1,
            grid=(tokens // BLOCK,),
            in_specs=[
                pl.BlockSpec((BLOCK, 2 * HEAD_DIM), lambda i, first: (i, 0)),
                pl.BlockSpec(key.shape, lambda i, first: (0, 0)),
                pl.BlockSpec(value.shape, lambda i, first: (0, 0)),
            ],
            out_specs=pl.BlockSpec((BLOCK, 2 * HEAD_DIM), lambda i, first: (i, 0)),
        ),
        out_shape=jax.ShapeDtypeStruct(query.shape, jnp.bfloat16),
        compiler_params=pltpu.CompilerParams(vmem_limit_bytes=VMEM_LIMIT),
        name="attend_all",
    )(first, query, key, value)


def scatter_kernel(shards, result, out, send, recv, own_sem):
    z = lax.axis_index("seq")
    rows, width = out.shape[0], result.shape[1]
    barrier = pltpu.get_barrier_semaphore()
    for d in range(1, shards):
        pl.semaphore_signal(
            barrier, inc=1, device_id={"seq": lax.rem(z + d, shards)}, device_id_type=MESH
        )
    pl.semaphore_wait(barrier, shards - 1)

    def columns(s):
        return out.at[:, pl.ds(pl.multiple_of(s * width, width), width)]

    def part(t):
        return result.at[pl.ds(pl.multiple_of(t * rows, rows), rows), :]

    def outgoing(d):
        t = lax.rem(z + d, shards)
        return remote(part(t), columns(z), send.at[d], recv.at[d], seq=t)

    def incoming(d):
        s = lax.rem(z + shards - d, shards)
        return remote(columns(s), columns(s), send.at[d], recv.at[d], seq=s)

    own = pltpu.make_async_copy(part(z), columns(z), own_sem)
    for d in range(1, shards):
        outgoing(d).start()
    own.start()
    for d in range(1, shards):
        incoming(d).wait_recv()
    own.wait()
    for d in range(1, shards):
        outgoing(d).wait_send()


def scatter_all(result, shards):
    tokens, width = result.shape
    dma = pltpu.SemaphoreType.DMA
    anywhere = pl.BlockSpec(memory_space=pl.ANY)
    return pl.pallas_call(
        functools.partial(scatter_kernel, shards),
        out_shape=jax.ShapeDtypeStruct((tokens // shards, width * shards), jnp.bfloat16),
        in_specs=[anywhere],
        out_specs=anywhere,
        scratch_shapes=[dma((shards,)), dma((shards,)), dma],
        compiler_params=pltpu.CompilerParams(collective_id=1, has_side_effects=True),
        name="scatter_all",
    )(result)


def rotation_tables(positions):
    half_dim = HEAD_DIM // 2
    frequency = ROPE_BASE ** (-(jnp.arange(half_dim, dtype=jnp.float32) * 2.0 / HEAD_DIM))
    angles = positions[:, None] * frequency[None, :]
    cosine, sine = jnp.cos(angles), jnp.sin(angles)
    return jnp.concatenate([cosine, cosine], axis=1), jnp.concatenate([-sine, sine], axis=1)


def by_heads(
    hidden, norm_gain, w_query, w_key, w_value, query_gain, key_gain, block_source, block_doc
):
    shards = lax.axis_size("seq")
    width = hidden.shape[1]
    blocks = block_source.shape[0]
    as_float = hidden.astype(jnp.float32)
    squares = jnp.sum(as_float * as_float, axis=1, keepdims=True)
    others = lax.ppermute(squares, "sub", [(0, 1), (1, 0)])
    gain = lax.dynamic_slice_in_dim(norm_gain, lax.axis_index("sub") * width, width)
    normed = (
        as_float * lax.rsqrt((squares + others) / (2 * width) + EPSILON) * gain[None, :]
    ).astype(jnp.bfloat16)
    first = jnp.sum((block_doc[None, :] < block_doc[:, None]).astype(jnp.int32), axis=1)
    cosine, sine = rotation_tables(
        token_positions(jnp.arange(blocks, dtype=jnp.int32), block_doc)
    )
    rows, weights = gather_all(normed, w_query, w_key, w_value, shards)
    per_shard = blocks // shards
    query, key, value = project_all(
        rows.reshape(shards, 2, per_shard, BLOCK, width),
        weights.reshape(2 * width, -1),
        jnp.stack([query_gain, key_gain]),
        cosine,
        sine,
        block_source,
        per_shard,
    )
    return scatter_all(attend_all(query, key, value, first), shards)


def fits(mesh):
    return (
        mesh.shape["groups"] == 2
        and mesh.shape["head"] == 2
        and mesh.shape["sub"] == 2
        and mesh.shape["seq"] == 4
    )


def solution(mesh):
    placed = (
        P(("groups", "seq"), "sub"),
        P(),
        P("seq", ("head", "sub")),
        P("seq", ("head", "sub")),
        P("seq", ("head", "sub")),
        P(),
        P(),
        P("groups"),
        P("groups"),
    )
    return jax.shard_map(
        by_heads if fits(mesh) else body,
        mesh=mesh,
        in_specs=placed,
        out_specs=P(("groups", "seq"), ("head", "sub")),
        check_vma=False,
    )
```

```python
import functools

import jax
import jax.numpy as jnp
import numpy as np
from jax import lax
from jax.experimental import pallas as pl
from jax.experimental.pallas import tpu as pltpu
from jax.sharding import PartitionSpec as P

HEAD_DIM = 128
WINDOW = 1024
BLOCK = 128
CAP = 2


QUERY_SCALE = 168.0 ** (-0.5)
EPSILON = 1e-06
ROPE_BASE = 10000.0


def passed_along(x, axis, by):
    size = lax.axis_size(axis)
    pairs = [(i, i + by) for i in range(size) if 0 <= i + by < size]
    return lax.ppermute(x, axis, pairs)


def table_lookup(table, indices):
    hits = indices[:, None] == jnp.arange(table.shape[0], dtype=jnp.int32)[None, :]
    return jnp.sum(jnp.where(hits, table[None, :], 0), axis=1)


def token_positions(block_ids, block_doc):
    first_block = jnp.sum((block_doc[None, :] < block_doc[:, None]).astype(jnp.int32), axis=1)
    start_block = table_lookup(first_block, block_ids)
    within = jnp.arange(BLOCK, dtype=jnp.int32)
    return (
        ((block_ids - start_block)[:, None] * BLOCK + within[None, :])
        .reshape(-1)
        .astype(jnp.float32)
    )


def token_docs(token_ids, block_doc):
    return table_lookup(block_doc, jnp.floor_divide(token_ids, BLOCK))


def head_rotation(values, gain, positions, factor):
    token_count = values.shape[0]
    per_head = values.reshape(token_count, -1, HEAD_DIM)
    normed = (
        per_head * lax.rsqrt(jnp.mean(per_head * per_head, axis=2, keepdims=True) + EPSILON) * gain
    )
    half_dim = HEAD_DIM // 2
    frequency = ROPE_BASE ** (-(jnp.arange(half_dim, dtype=jnp.float32) * 2.0 / HEAD_DIM))
    angles = positions[:, None] * frequency[None, :]
    cosine = jnp.cos(angles)[:, None, :]
    sine_table = jnp.sin(angles)[:, None, :]
    first_half = normed[:, :, :half_dim]
    second_half = normed[:, :, half_dim:]
    turned = jnp.concatenate(
        [
            first_half * cosine - second_half * sine_table,
            second_half * cosine + first_half * sine_table,
        ],
        axis=2,
    )
    return (turned * factor).reshape(token_count, -1).astype(jnp.bfloat16)


def side_ranks(labels):
    length = labels.shape[0]
    earlier = jnp.arange(length)[None, :] < jnp.arange(length)[:, None]
    matching = labels[None, :] == labels[:, None]
    return jnp.sum((earlier & matching).astype(jnp.int32), axis=1)


def outgoing_slots(block_source, target, own_shard, block_count, shard_count):
    first_slot = jnp.clip(target, 0, shard_count - 1) * block_count
    slot_ids = lax.dynamic_slice_in_dim(block_source, first_slot, block_count)
    sending = (slot_ids // block_count == own_shard) & (target >= 0) & (target < shard_count)
    send_rank = side_ranks(sending.astype(jnp.int32))
    wanted = (jnp.arange(CAP)[:, None] == send_rank[None, :]) & sending[None, :]
    return jnp.sum(jnp.where(wanted, (slot_ids % block_count)[None, :], 0), axis=1)


def incoming_index(block_source, own_shard, block_count):
    slot_ids = lax.dynamic_slice_in_dim(block_source, own_shard * block_count, block_count)
    sides = slot_ids // block_count - own_shard
    side_rank = side_ranks(sides)
    from_prior = block_count + side_rank
    from_next = block_count + CAP + side_rank
    return jnp.where(
        sides == 0, slot_ids % block_count, jnp.where(sides < 0, from_prior, from_next)
    )


def blocks_at(pieces, chosen):
    picked = [
        lax.dynamic_slice_in_dim(pieces, chosen[i], 1, 0) for i in range(chosen.shape[0])
    ]
    return jnp.concatenate(picked, axis=0)


def migrate(values, block_source, own_shard, shard_count):
    row_count, col_count = values.shape
    block_count = row_count // BLOCK
    pieces = values.reshape(block_count, BLOCK, col_count)
    block_pool = [pieces]
    for offset in (1, -1):
        chosen = outgoing_slots(
            block_source, own_shard + offset, own_shard, block_count, shard_count
        )
        outgoing = blocks_at(pieces, chosen)
        block_pool.append(passed_along(outgoing, "seq", offset))
    joined = jnp.concatenate(block_pool, axis=0)
    placed = blocks_at(joined, incoming_index(block_source, own_shard, block_count))
    return placed.reshape(row_count, col_count)


def gathered(x, axis, dim):
    size = lax.axis_size(axis)
    index = lax.axis_index(axis)
    extent = x.shape[dim]
    shape = list(x.shape)
    shape[dim] = extent * size
    whole = jnp.zeros(shape, x.dtype)
    pairs = [(i, (i + 1) % size) for i in range(size)]
    for step in range(size):
        owner = lax.rem(index + size - step, size)
        whole = lax.dynamic_update_slice_in_dim(whole, x, owner * extent, dim)
        if step < size - 1:
            x = lax.ppermute(x, axis, pairs)
    return whole


def project_rows(halves, norm_gain, w_query, w_key, w_value, query_gain, key_gain, positions):
    full_rows = gathered(halves, "sub", 1)
    as_float = full_rows.astype(jnp.float32)
    normed = (
        as_float
        * lax.rsqrt(jnp.mean(as_float * as_float, axis=1, keepdims=True) + EPSILON)
        * norm_gain
    ).astype(jnp.bfloat16)
    segments = (
        gathered(w_query, "seq", 0),
        gathered(w_key, "seq", 0),
        gathered(w_value, "seq", 0),
    )
    query_raw, key_raw, value_raw = tuple(
        (jnp.dot(normed, segment, preferred_element_type=jnp.float32) for segment in segments)
    )
    query_rot = head_rotation(query_raw, query_gain, positions, QUERY_SCALE)
    key_rot = head_rotation(key_raw, key_gain, positions, 1.0)
    return jnp.concatenate([query_rot, key_rot, value_raw.astype(jnp.bfloat16)], axis=1)


def attend_block(query_rows, key_rows, value_rows, query_tokens, key_tokens, query_docs, key_docs):
    query_count = query_rows.shape[0]
    key_count = key_rows.shape[0]
    kv_count = key_rows.shape[1] // HEAD_DIM
    query_heads = query_rows.reshape(query_count, kv_count, 2, HEAD_DIM)
    key_heads = key_rows.reshape(key_count, kv_count, HEAD_DIM)
    value_heads = value_rows.reshape(key_count, kv_count, HEAD_DIM)
    scores = jnp.einsum(
        "qgjd,kgd->gjqk", query_heads, key_heads, preferred_element_type=jnp.float32
    )
    allowed = (key_tokens[None, :] >= 0) & (key_tokens[None, :] <= query_tokens[:, None])
    allowed = (
        allowed
        & (query_tokens[:, None] - key_tokens[None, :] < WINDOW)
        & (key_docs[None, :] == query_docs[:, None])
    )
    weight_exp = jnp.where(allowed, jnp.exp(scores), 0.0)
    totals = jnp.sum(weight_exp, axis=3)
    summed = jnp.einsum(
        "gjqk,kgd->qgjd",
        weight_exp.astype(jnp.bfloat16),
        value_heads,
        preferred_element_type=jnp.float32,
    )
    return (
        (summed / jnp.transpose(totals, (2, 0, 1))[:, :, :, None])
        .reshape(query_count, -1)
        .astype(jnp.bfloat16)
    )


def body(hidden, norm_gain, w_query, w_key, w_value, query_gain, key_gain, block_source, block_doc):
    row_count = hidden.shape[0]
    block_count = row_count // BLOCK
    own_shard = lax.axis_index("seq")
    shard_count = lax.axis_size("seq")
    own_blocks = own_shard * block_count + jnp.arange(block_count, dtype=jnp.int32)
    moved = migrate(hidden, block_source, own_shard, shard_count)
    packed = project_rows(
        moved,
        norm_gain,
        w_query,
        w_key,
        w_value,
        query_gain,
        key_gain,
        token_positions(own_blocks, block_doc),
    )
    query_width = w_query.shape[1]
    key_width = w_key.shape[1]
    query_rot = packed[:, :query_width]
    key_value = packed[:, query_width:]
    halo_count = max(1, WINDOW // row_count)
    received = []
    for distance in range(halo_count, 0, -1):
        received.append(passed_along(key_value, "seq", distance))
    extended = jnp.concatenate(received + [key_value], axis=0)
    key_all = extended[:, :key_width]
    value_all = extended[:, key_width:]
    query_tokens = own_shard * row_count + jnp.arange(row_count, dtype=jnp.int32)
    key_tokens = own_shard * row_count - WINDOW + jnp.arange(extended.shape[0], dtype=jnp.int32)
    query_docs = token_docs(query_tokens, block_doc)
    key_docs = token_docs(key_tokens, block_doc)
    block_rows = min(512, row_count)

    def one_block(block_index):
        return attend_block(
            query_rot, key_all, value_all, query_tokens, key_tokens, query_docs, key_docs
        )

    result = lax.map(one_block, jnp.arange(row_count // block_rows, dtype=jnp.int32))
    return result.reshape(row_count, -1)


MESH = pl.DeviceIdType.MESH
CHUNKS = 4
VMEM_LIMIT = 48 * 1024 * 1024


def remote(src, dst, send_sem, recv_sem, **target):
    return pltpu.make_async_remote_copy(
        src_ref=src,
        dst_ref=dst,
        send_sem=send_sem,
        recv_sem=recv_sem,
        device_id=target,
        device_id_type=MESH,
    )


def gather_kernel(
    shards, hidden, norm_gain, gains, block_turn, within_turn, wq, wk, wv, out,
    rows, weights, mine, theirs,
    zr_send, zr_recv, zl_send, zl_recv, x_send, x_recv, c_send, c_recv,
    w_send, w_recv, y_send, y_recv, ownw_sem, s_send, s_recv,
):
    y, z = lax.axis_index("groups"), lax.axis_index("seq")
    x, c = lax.axis_index("head"), lax.axis_index("sub")
    chunks, chunk, width = hidden.shape[1:]
    widths = (wq.shape[2] // shards, wk.shape[2] // shards, wv.shape[2] // shards)
    starts = (0, widths[0], widths[0] + widths[1])

    barrier = pltpu.get_barrier_semaphore()
    for d in range(1, shards):
        pl.semaphore_signal(
            barrier, inc=1, device_id={"seq": lax.rem(z + d, shards)}, device_id_type=MESH
        )
    pl.semaphore_signal(barrier, inc=1, device_id={"groups": 1 - y}, device_id_type=MESH)
    pl.semaphore_signal(barrier, inc=1, device_id={"head": 1 - x}, device_id_type=MESH)
    pl.semaphore_signal(barrier, inc=1, device_id={"sub": 1 - c}, device_id_type=MESH)
    pl.semaphore_wait(barrier, shards + 2)

    def along(step, j, right):
        s = z - step if right else z + step
        send, recv = (zr_send, zr_recv) if right else (zl_send, zl_recv)
        return remote(
            rows.at[s, c, x, j], rows.at[s, c, x, j], send.at[step, j], recv.at[step + 1, j],
            seq=z + 1 if right else z - 1,
        )

    def along_recv(step, j, right):
        s = z - step if right else z + step
        send, recv = (zr_send, zr_recv) if right else (zl_send, zl_recv)
        return remote(
            rows.at[s, c, x, j], rows.at[s, c, x, j], send.at[0, j], recv.at[step, j],
            seq=z - 1 if right else z + 1,
        )

    def across(s, j, half):
        return remote(
            rows.at[s, c, half, j], rows.at[s, c, half, j], x_send.at[s, j], x_recv.at[s, j],
            head=1 - x,
        )

    def to_core(s, half, j):
        where = rows.at[s, c, half, j]
        return remote(where, where, c_send.at[s, half, j], c_recv.at[s, half, j], sub=1 - c)

    def from_core(s, half, j):
        where = rows.at[s, 1 - c, half, j]
        return remote(where, where, c_send.at[s, half, j], c_recv.at[s, half, j], sub=1 - c)

    def weight_piece(d, n):
        t = lax.rem(z + d, shards)
        src = (wq, wk, wv)[n].at[y, :, pl.ds(pl.multiple_of(t * widths[n], widths[n]), widths[n])]
        return remote(
            src, weights.at[z, y, :, pl.ds(starts[n], widths[n])],
            w_send.at[d, n], w_recv.at[d, n], seq=t,
        )

    def weight_arrival(d, n):
        s = lax.rem(z + shards - d, shards)
        where = weights.at[s, y, :, pl.ds(starts[n], widths[n])]
        return remote(where, where, w_send.at[d, n], w_recv.at[d, n], seq=s)

    def weight_across(d, half):
        s = lax.rem(z + shards - d, shards)
        where = weights.at[s, half]
        return remote(where, where, y_send.at[d], y_recv.at[d], groups=1 - y)

    def own_weight(n):
        src = (wq, wk, wv)[n].at[:, :, pl.ds(pl.multiple_of(z * widths[n], widths[n]), widths[n])]
        return pltpu.make_async_copy(
            src, weights.at[z, :, :, pl.ds(starts[n], widths[n])], ownw_sem.at[n]
        )

    def sums():
        return remote(mine, theirs, s_send, s_recv, sub=1 - c)

    for d in range(1, shards):
        for n in range(3):
            weight_piece(d, n).start()
    for n in range(3):
        own_weight(n).start()

    def add_up(i, _):
        half, j = i // chunks, i % chunks
        values = hidden[half, j].astype(jnp.float32)
        total = jnp.sum(values * values, axis=1, keepdims=True)
        mine[half, j] = jnp.broadcast_to(total, (chunk, HEAD_DIM))
        return 0

    lax.fori_loop(0, 2 * chunks, add_up, 0)
    sums().start()
    sums().wait_recv()

    def normalise(i, _):
        half, j = (x + i // chunks) % 2, i % chunks
        mean = (mine[half, j][:, :1] + theirs[half, j][:, :1]) / (2 * width)
        values = hidden[half, j].astype(jnp.float32) * lax.rsqrt(mean + EPSILON)
        rows[z, c, half, j] = (values * norm_gain[pl.ds(c, 1), :]).astype(jnp.bfloat16)
        for right in (True, False):

            @pl.when((i < chunks) & (z + 1 < shards if right else z > 0))
            def _():
                along(0, j, right).start()

        to_core(z, half, j).start()
        return 0

    lax.fori_loop(0, 2 * chunks, normalise, 0)

    def has(step, right):
        return z - step >= 0 if right else z + step < shards

    def second_hop(step, j):
        for right in (True, False):

            @pl.when(has(step, right))
            def _():
                s = z - step if right else z + step
                across(s, j, 1 - x).wait_recv()
                to_core(s, 1 - x, j).start()

    def handle(step, j):
        for right in (True, False):

            @pl.when(has(step, right))
            def _():
                s = z - step if right else z + step
                along_recv(step, j, right).wait_recv()

                @pl.when(z + 1 < shards if right else z > 0)
                def _():
                    along(step, j, right).start()

                across(s, j, x).start()
                to_core(s, x, j).start()

    def swap_weights(d):
        for n in range(3):
            weight_arrival(d, n).wait_recv()
        weight_across(d, y).start()

    def turned(u, gain, cosine, sine, factor):
        n = u * lax.rsqrt(jnp.mean(u * u, axis=1, keepdims=True) + EPSILON) * gain
        swapped = pltpu.roll(n, HEAD_DIM // 2, 1)
        return ((n * cosine + swapped * sine) * factor).astype(jnp.bfloat16)

    def project(i):
        m, half = i // 2, i % 2
        s = ((z // 2 + m // 2) % 2) * 2 + (z % 2 + m % 2) % 2
        for j in range(chunks):
            from_core(s, half, j).wait_recv()
        acc = jnp.zeros((2 * BLOCK, 4 * HEAD_DIM), jnp.float32)
        for part in range(2):
            left = rows[s, part, half].reshape(2 * BLOCK, width)
            right = weights[part * shards // 2 : (part + 1) * shards // 2]
            acc = acc + jnp.dot(
                left, right.reshape(width, 4 * HEAD_DIM), preferred_element_type=jnp.float32
            )
        for block in range(2):
            slot = s * 4 + half * 2 + block
            bc, bs = block_turn[0, pl.ds(slot, 1), :], block_turn[1, pl.ds(slot, 1), :]
            wc, ws = within_turn[0], within_turn[1]
            lane = lax.broadcasted_iota(jnp.int32, (BLOCK, HEAD_DIM), 1)
            cosine = bc * wc - bs * ws
            sine = jnp.where(lane < HEAD_DIM // 2, -1.0, 1.0) * (bs * wc + bc * ws)
            at = pl.ds(pl.multiple_of(slot * BLOCK, BLOCK), BLOCK)
            own = acc[block * BLOCK : (block + 1) * BLOCK]
            for h in range(3):
                cols = slice(h * HEAD_DIM, (h + 1) * HEAD_DIM)
                gain, factor = (gains[0:1], QUERY_SCALE) if h < 2 else (gains[1:2], 1.0)
                out[at, cols] = turned(own[:, cols], gain, cosine, sine, factor)
            out[at, 3 * HEAD_DIM :] = own[:, 3 * HEAD_DIM :].astype(jnp.bfloat16)

    for j in range(chunks):
        handle(1, j)
        if j > 0:
            second_hop(1, j - 1)
    swap_weights(1)

    for n in range(2 * chunks + 2):
        if n < 2 * chunks:
            handle(2 + n // chunks, n % chunks)
        if n < 2:
            swap_weights(2 + n)
        if n == 0:
            second_hop(1, chunks - 1)
        elif n <= 2 * chunks:
            second_hop(2 + (n - 1) // chunks, (n - 1) % chunks)
        if n == 2:
            for d in range(1, shards):
                weight_across(d, 1 - y).wait_recv()
            for k in range(3):
                own_weight(k).wait()
        if n >= 2:
            project(n - 2)

    sums().wait_send()
    for d in range(1, shards):
        for n in range(3):
            weight_piece(d, n).wait_send()
        weight_across(d, y).wait_send()
    for step in range(shards):
        for right in (True, False):

            @pl.when(has(step, right) & (z + 1 < shards if right else z > 0))
            def _():
                for j in range(chunks):
                    along(step, j, right).wait_send()

            if step > 0:

                @pl.when(has(step, right))
                def _():
                    s = z - step if right else z + step
                    for j in range(chunks):
                        across(s, j, x).wait_send()
    for s in range(shards):
        for half in range(2):
            for j in range(chunks):
                to_core(s, half, j).wait_send()


def gather_all(hidden, norm_gain, gains, block_turn, within_turn, w_query, w_key, w_value, shards):
    row_count, width = hidden.shape
    depth = w_query.shape[0]
    chunk = row_count // (2 * CHUNKS)
    total = (w_query.shape[1] + w_key.shape[1] + w_value.shape[1]) // shards
    halves = [w.reshape(2, depth // 2, w.shape[1]) for w in (w_query, w_key, w_value)]
    dma = pltpu.SemaphoreType.DMA
    line = dma((shards + 1, CHUNKS))
    anywhere = pl.BlockSpec(memory_space=pl.ANY)
    inside = pl.BlockSpec(memory_space=pltpu.VMEM)
    return pl.pallas_call(
        functools.partial(gather_kernel, shards),
        out_shape=jax.ShapeDtypeStruct((row_count * shards, total), jnp.bfloat16),
        in_specs=[inside] * 5 + [anywhere] * 3,
        out_specs=inside,
        scratch_shapes=[
            pltpu.VMEM((shards, 2, 2, CHUNKS, chunk, width), jnp.bfloat16),
            pltpu.VMEM((shards, 2, depth // 2, total), jnp.bfloat16),
            pltpu.VMEM((2, CHUNKS, chunk, HEAD_DIM), jnp.float32),
            pltpu.VMEM((2, CHUNKS, chunk, HEAD_DIM), jnp.float32),
            line, line, line, line, line, line,
            dma((shards, 2, CHUNKS)), dma((shards, 2, CHUNKS)),
            dma((shards, 3)), dma((shards, 3)), dma((shards,)), dma((shards,)),
            dma((3,)), dma, dma,
        ],
        compiler_params=pltpu.CompilerParams(
            collective_id=0, has_side_effects=True, vmem_limit_bytes=VMEM_LIMIT
        ),
        name="gather_all",
    )(
        hidden.reshape(2, CHUNKS, chunk, width), norm_gain.reshape(2, width), gains,
        block_turn, within_turn, *halves,
    )


def attend_kernel(first, source, q_ref, all_ref, out_ref, k_ref, v_ref):
    b = pl.program_id(0)

    @pl.when(b == 0)
    def _():
        for i in range(k_ref.shape[0] // BLOCK):
            at = pl.ds(pl.multiple_of(source[i] * BLOCK, BLOCK), BLOCK)
            k_ref[i * BLOCK : (i + 1) * BLOCK, :] = all_ref[at, 2 * HEAD_DIM : 3 * HEAD_DIM]
            v_ref[i * BLOCK : (i + 1) * BLOCK, :] = all_ref[at, 3 * HEAD_DIM :]

    span = 2 * BLOCK
    query = jnp.concatenate([q_ref[:, :HEAD_DIM], q_ref[:, HEAD_DIM:]], axis=0)
    start = first[b] * BLOCK
    lowest = jnp.maximum(first[b], b - WINDOW // BLOCK)
    token = b * BLOCK + lax.rem(lax.broadcasted_iota(jnp.int32, (span, span), 0), BLOCK)
    lane = lax.broadcasted_iota(jnp.int32, (span, span), 1)
    least = jnp.maximum(start, token - (WINDOW - 1))

    def step(i, carry):
        acc, total = carry
        at = pl.multiple_of(i * span, span)
        keys = k_ref[pl.ds(at, span), :]
        scores = lax.dot_general(
            query, keys, (((1,), (1,)), ((), ())), preferred_element_type=jnp.float32
        )
        other = lane + at
        allowed = (other <= token) & (other >= least)
        weight = jnp.where(allowed, jnp.exp(scores), 0.0)
        total = total + weight[:, :HEAD_DIM] + weight[:, HEAD_DIM:]
        acc = acc + jnp.dot(
            weight.astype(jnp.bfloat16),
            v_ref[pl.ds(at, span), :],
            preferred_element_type=jnp.float32,
        )
        return acc, total

    zero = jnp.zeros((span, HEAD_DIM), jnp.float32)
    acc, total = lax.fori_loop(lowest // 2, b // 2 + 1, step, (zero, zero))
    result = (acc / jnp.sum(total, axis=1, keepdims=True)).astype(jnp.bfloat16)
    out_ref[:, :HEAD_DIM] = result[:BLOCK]
    out_ref[:, HEAD_DIM:] = result[BLOCK:]


def attend_all(packed, first, source):
    tokens = packed.shape[0]
    return pl.pallas_call(
        attend_kernel,
        grid_spec=pltpu.PrefetchScalarGridSpec(
            num_scalar_prefetch=2,
            grid=(tokens // BLOCK,),
            in_specs=[
                pl.BlockSpec((BLOCK, 2 * HEAD_DIM), lambda i, first, source: (source[i], 0)),
                pl.BlockSpec(packed.shape, lambda i, first, source: (0, 0)),
            ],
            out_specs=pl.BlockSpec((BLOCK, 2 * HEAD_DIM), lambda i, first, source: (i, 0)),
            scratch_shapes=[
                pltpu.VMEM((tokens, HEAD_DIM), jnp.bfloat16),
                pltpu.VMEM((tokens, HEAD_DIM), jnp.bfloat16),
            ],
        ),
        out_shape=jax.ShapeDtypeStruct((tokens, 2 * HEAD_DIM), jnp.bfloat16),
        compiler_params=pltpu.CompilerParams(vmem_limit_bytes=VMEM_LIMIT),
        name="attend_all",
    )(first, source, packed, packed)


def scatter_kernel(shards, result, out, send, recv, own_sem):
    z = lax.axis_index("seq")
    rows, width = out.shape[0], result.shape[1]
    barrier = pltpu.get_barrier_semaphore()
    for d in range(1, shards):
        pl.semaphore_signal(
            barrier, inc=1, device_id={"seq": lax.rem(z + d, shards)}, device_id_type=MESH
        )
    pl.semaphore_wait(barrier, shards - 1)

    def columns(s):
        return out.at[:, pl.ds(pl.multiple_of(s * width, width), width)]

    def part(t):
        return result.at[pl.ds(pl.multiple_of(t * rows, rows), rows), :]

    def outgoing(d):
        t = lax.rem(z + d, shards)
        return remote(part(t), columns(z), send.at[d], recv.at[d], seq=t)

    def incoming(d):
        s = lax.rem(z + shards - d, shards)
        return remote(columns(s), columns(s), send.at[d], recv.at[d], seq=s)

    own = pltpu.make_async_copy(part(z), columns(z), own_sem)
    for d in range(1, shards):
        outgoing(d).start()
    own.start()
    for d in range(1, shards):
        incoming(d).wait_recv()
    own.wait()
    for d in range(1, shards):
        outgoing(d).wait_send()


def scatter_all(result, shards):
    tokens, width = result.shape
    dma = pltpu.SemaphoreType.DMA
    anywhere = pl.BlockSpec(memory_space=pl.ANY)
    return pl.pallas_call(
        functools.partial(scatter_kernel, shards),
        out_shape=jax.ShapeDtypeStruct((tokens // shards, width * shards), jnp.bfloat16),
        in_specs=[anywhere],
        out_specs=anywhere,
        scratch_shapes=[dma((shards,)), dma((shards,)), dma],
        compiler_params=pltpu.CompilerParams(collective_id=1, has_side_effects=True),
        name="scatter_all",
    )(result)


def turn_table(positions):
    half_dim = HEAD_DIM // 2
    frequency = ROPE_BASE ** (-(np.arange(half_dim, dtype=np.float64) * 2.0 / HEAD_DIM))
    angles = np.asarray(positions, np.float64)[:, None] * np.tile(frequency, 2)[None, :]
    return np.stack([np.cos(angles), np.sin(angles)]).astype(np.float32)


def by_heads(
    hidden, norm_gain, w_query, w_key, w_value, query_gain, key_gain, block_source, block_doc
):
    shards = lax.axis_size("seq")
    blocks = block_source.shape[0]
    ids = jnp.arange(blocks, dtype=jnp.int32)
    first = jnp.sum((block_doc[None, :] < block_doc[:, None]).astype(jnp.int32), axis=1)
    arrived = block_source[None, :] == ids[:, None]
    offset = jnp.sum(jnp.where(arrived, (ids - first)[None, :], 0), axis=1)
    picked = (offset[:, None] == ids[None, :])[None, :, :, None]
    table = jnp.asarray(turn_table(np.arange(blocks) * BLOCK))
    block_turn = jnp.sum(jnp.where(picked, table[:, None, :, :], 0.0), axis=2)
    packed = gather_all(
        hidden,
        norm_gain,
        jnp.stack([query_gain, key_gain]),
        block_turn,
        jnp.asarray(turn_table(np.arange(BLOCK))),
        w_query,
        w_key,
        w_value,
        shards,
    )
    return scatter_all(attend_all(packed, first, block_source), shards)


def fits(mesh):
    return (
        mesh.shape["groups"] == 2
        and mesh.shape["head"] == 2
        and mesh.shape["sub"] == 2
        and mesh.shape["seq"] == 4
    )


def solution(mesh):
    placed = (
        P(("groups", "seq"), "sub"),
        P(),
        P("seq", ("head", "sub")),
        P("seq", ("head", "sub")),
        P("seq", ("head", "sub")),
        P(),
        P(),
        P("groups"),
        P("groups"),
    )
    return jax.shard_map(
        by_heads if fits(mesh) else body,
        mesh=mesh,
        in_specs=placed,
        out_specs=P(("groups", "seq"), ("head", "sub")),
        check_vma=False,
    )
```

```python
import functools

import jax
import jax.numpy as jnp
import numpy as np
from jax import lax
from jax.experimental import pallas as pl
from jax.experimental.pallas import tpu as pltpu
from jax.sharding import PartitionSpec as P

HEAD_DIM = 128
WINDOW = 1024
BLOCK = 128
CAP = 2


QUERY_SCALE = 168.0 ** (-0.5)
EPSILON = 1e-06
ROPE_BASE = 10000.0


def passed_along(x, axis, by):
    size = lax.axis_size(axis)
    pairs = [(i, i + by) for i in range(size) if 0 <= i + by < size]
    return lax.ppermute(x, axis, pairs)


def table_lookup(table, indices):
    hits = indices[:, None] == jnp.arange(table.shape[0], dtype=jnp.int32)[None, :]
    return jnp.sum(jnp.where(hits, table[None, :], 0), axis=1)


def token_positions(block_ids, block_doc):
    first_block = jnp.sum((block_doc[None, :] < block_doc[:, None]).astype(jnp.int32), axis=1)
    start_block = table_lookup(first_block, block_ids)
    within = jnp.arange(BLOCK, dtype=jnp.int32)
    return (
        ((block_ids - start_block)[:, None] * BLOCK + within[None, :])
        .reshape(-1)
        .astype(jnp.float32)
    )


def token_docs(token_ids, block_doc):
    return table_lookup(block_doc, jnp.floor_divide(token_ids, BLOCK))


def head_rotation(values, gain, positions, factor):
    token_count = values.shape[0]
    per_head = values.reshape(token_count, -1, HEAD_DIM)
    normed = (
        per_head * lax.rsqrt(jnp.mean(per_head * per_head, axis=2, keepdims=True) + EPSILON) * gain
    )
    half_dim = HEAD_DIM // 2
    frequency = ROPE_BASE ** (-(jnp.arange(half_dim, dtype=jnp.float32) * 2.0 / HEAD_DIM))
    angles = positions[:, None] * frequency[None, :]
    cosine = jnp.cos(angles)[:, None, :]
    sine_table = jnp.sin(angles)[:, None, :]
    first_half = normed[:, :, :half_dim]
    second_half = normed[:, :, half_dim:]
    turned = jnp.concatenate(
        [
            first_half * cosine - second_half * sine_table,
            second_half * cosine + first_half * sine_table,
        ],
        axis=2,
    )
    return (turned * factor).reshape(token_count, -1).astype(jnp.bfloat16)


def side_ranks(labels):
    length = labels.shape[0]
    earlier = jnp.arange(length)[None, :] < jnp.arange(length)[:, None]
    matching = labels[None, :] == labels[:, None]
    return jnp.sum((earlier & matching).astype(jnp.int32), axis=1)


def outgoing_slots(block_source, target, own_shard, block_count, shard_count):
    first_slot = jnp.clip(target, 0, shard_count - 1) * block_count
    slot_ids = lax.dynamic_slice_in_dim(block_source, first_slot, block_count)
    sending = (slot_ids // block_count == own_shard) & (target >= 0) & (target < shard_count)
    send_rank = side_ranks(sending.astype(jnp.int32))
    wanted = (jnp.arange(CAP)[:, None] == send_rank[None, :]) & sending[None, :]
    return jnp.sum(jnp.where(wanted, (slot_ids % block_count)[None, :], 0), axis=1)


def incoming_index(block_source, own_shard, block_count):
    slot_ids = lax.dynamic_slice_in_dim(block_source, own_shard * block_count, block_count)
    sides = slot_ids // block_count - own_shard
    side_rank = side_ranks(sides)
    from_prior = block_count + side_rank
    from_next = block_count + CAP + side_rank
    return jnp.where(
        sides == 0, slot_ids % block_count, jnp.where(sides < 0, from_prior, from_next)
    )


def blocks_at(pieces, chosen):
    picked = [
        lax.dynamic_slice_in_dim(pieces, chosen[i], 1, 0) for i in range(chosen.shape[0])
    ]
    return jnp.concatenate(picked, axis=0)


def migrate(values, block_source, own_shard, shard_count):
    row_count, col_count = values.shape
    block_count = row_count // BLOCK
    pieces = values.reshape(block_count, BLOCK, col_count)
    block_pool = [pieces]
    for offset in (1, -1):
        chosen = outgoing_slots(
            block_source, own_shard + offset, own_shard, block_count, shard_count
        )
        outgoing = blocks_at(pieces, chosen)
        block_pool.append(passed_along(outgoing, "seq", offset))
    joined = jnp.concatenate(block_pool, axis=0)
    placed = blocks_at(joined, incoming_index(block_source, own_shard, block_count))
    return placed.reshape(row_count, col_count)


def gathered(x, axis, dim):
    size = lax.axis_size(axis)
    index = lax.axis_index(axis)
    extent = x.shape[dim]
    shape = list(x.shape)
    shape[dim] = extent * size
    whole = jnp.zeros(shape, x.dtype)
    pairs = [(i, (i + 1) % size) for i in range(size)]
    for step in range(size):
        owner = lax.rem(index + size - step, size)
        whole = lax.dynamic_update_slice_in_dim(whole, x, owner * extent, dim)
        if step < size - 1:
            x = lax.ppermute(x, axis, pairs)
    return whole


def project_rows(halves, norm_gain, w_query, w_key, w_value, query_gain, key_gain, positions):
    full_rows = gathered(halves, "sub", 1)
    as_float = full_rows.astype(jnp.float32)
    normed = (
        as_float
        * lax.rsqrt(jnp.mean(as_float * as_float, axis=1, keepdims=True) + EPSILON)
        * norm_gain
    ).astype(jnp.bfloat16)
    segments = (
        gathered(w_query, "seq", 0),
        gathered(w_key, "seq", 0),
        gathered(w_value, "seq", 0),
    )
    query_raw, key_raw, value_raw = tuple(
        (jnp.dot(normed, segment, preferred_element_type=jnp.float32) for segment in segments)
    )
    query_rot = head_rotation(query_raw, query_gain, positions, QUERY_SCALE)
    key_rot = head_rotation(key_raw, key_gain, positions, 1.0)
    return jnp.concatenate([query_rot, key_rot, value_raw.astype(jnp.bfloat16)], axis=1)


def attend_block(query_rows, key_rows, value_rows, query_tokens, key_tokens, query_docs, key_docs):
    query_count = query_rows.shape[0]
    key_count = key_rows.shape[0]
    kv_count = key_rows.shape[1] // HEAD_DIM
    query_heads = query_rows.reshape(query_count, kv_count, 2, HEAD_DIM)
    key_heads = key_rows.reshape(key_count, kv_count, HEAD_DIM)
    value_heads = value_rows.reshape(key_count, kv_count, HEAD_DIM)
    scores = jnp.einsum(
        "qgjd,kgd->gjqk", query_heads, key_heads, preferred_element_type=jnp.float32
    )
    allowed = (key_tokens[None, :] >= 0) & (key_tokens[None, :] <= query_tokens[:, None])
    allowed = (
        allowed
        & (query_tokens[:, None] - key_tokens[None, :] < WINDOW)
        & (key_docs[None, :] == query_docs[:, None])
    )
    weight_exp = jnp.where(allowed, jnp.exp(scores), 0.0)
    totals = jnp.sum(weight_exp, axis=3)
    summed = jnp.einsum(
        "gjqk,kgd->qgjd",
        weight_exp.astype(jnp.bfloat16),
        value_heads,
        preferred_element_type=jnp.float32,
    )
    return (
        (summed / jnp.transpose(totals, (2, 0, 1))[:, :, :, None])
        .reshape(query_count, -1)
        .astype(jnp.bfloat16)
    )


def body(hidden, norm_gain, w_query, w_key, w_value, query_gain, key_gain, block_source, block_doc):
    row_count = hidden.shape[0]
    block_count = row_count // BLOCK
    own_shard = lax.axis_index("seq")
    shard_count = lax.axis_size("seq")
    own_blocks = own_shard * block_count + jnp.arange(block_count, dtype=jnp.int32)
    moved = migrate(hidden, block_source, own_shard, shard_count)
    packed = project_rows(
        moved,
        norm_gain,
        w_query,
        w_key,
        w_value,
        query_gain,
        key_gain,
        token_positions(own_blocks, block_doc),
    )
    query_width = w_query.shape[1]
    key_width = w_key.shape[1]
    query_rot = packed[:, :query_width]
    key_value = packed[:, query_width:]
    halo_count = max(1, WINDOW // row_count)
    received = []
    for distance in range(halo_count, 0, -1):
        received.append(passed_along(key_value, "seq", distance))
    extended = jnp.concatenate(received + [key_value], axis=0)
    key_all = extended[:, :key_width]
    value_all = extended[:, key_width:]
    query_tokens = own_shard * row_count + jnp.arange(row_count, dtype=jnp.int32)
    key_tokens = own_shard * row_count - WINDOW + jnp.arange(extended.shape[0], dtype=jnp.int32)
    query_docs = token_docs(query_tokens, block_doc)
    key_docs = token_docs(key_tokens, block_doc)
    block_rows = min(512, row_count)

    def one_block(block_index):
        return attend_block(
            query_rot, key_all, value_all, query_tokens, key_tokens, query_docs, key_docs
        )

    result = lax.map(one_block, jnp.arange(row_count // block_rows, dtype=jnp.int32))
    return result.reshape(row_count, -1)


MESH = pl.DeviceIdType.MESH
CHUNKS = 4
VMEM_LIMIT = 48 * 1024 * 1024


def remote(src, dst, send_sem, recv_sem, **target):
    return pltpu.make_async_remote_copy(
        src_ref=src,
        dst_ref=dst,
        send_sem=send_sem,
        recv_sem=recv_sem,
        device_id=target,
        device_id_type=MESH,
    )


def gather_kernel(
    shards, hidden, norm_gain, gains, block_turn, within_turn, wq, wk, wv, out,
    rows, weights, mine, theirs,
    zr_send, zr_recv, zl_send, zl_recv, x_send, x_recv, c_send, c_recv,
    w_send, w_recv, y_send, y_recv, ownw_sem, s_send, s_recv,
):
    y, z = lax.axis_index("groups"), lax.axis_index("seq")
    x, c = lax.axis_index("head"), lax.axis_index("sub")
    chunks, chunk, width = hidden.shape[1:]
    widths = (wq.shape[2] // shards, wk.shape[2] // shards, wv.shape[2] // shards)
    starts = (0, widths[0], widths[0] + widths[1])

    barrier = pltpu.get_barrier_semaphore()
    for d in range(1, shards):
        pl.semaphore_signal(
            barrier, inc=1, device_id={"seq": lax.rem(z + d, shards)}, device_id_type=MESH
        )
    pl.semaphore_signal(barrier, inc=1, device_id={"groups": 1 - y}, device_id_type=MESH)
    pl.semaphore_signal(barrier, inc=1, device_id={"head": 1 - x}, device_id_type=MESH)
    pl.semaphore_signal(barrier, inc=1, device_id={"sub": 1 - c}, device_id_type=MESH)
    pl.semaphore_wait(barrier, shards + 2)

    def along(step, j, right):
        s = z - step if right else z + step
        send, recv = (zr_send, zr_recv) if right else (zl_send, zl_recv)
        return remote(
            rows.at[s, c, x, j], rows.at[s, c, x, j], send.at[step, j], recv.at[step + 1, j],
            seq=z + 1 if right else z - 1,
        )

    def along_recv(step, j, right):
        s = z - step if right else z + step
        send, recv = (zr_send, zr_recv) if right else (zl_send, zl_recv)
        return remote(
            rows.at[s, c, x, j], rows.at[s, c, x, j], send.at[0, j], recv.at[step, j],
            seq=z - 1 if right else z + 1,
        )

    def across(s, j, half):
        return remote(
            rows.at[s, c, half, j], rows.at[s, c, half, j], x_send.at[s, j], x_recv.at[s, j],
            head=1 - x,
        )

    def to_core(s, half, j):
        where = rows.at[s, c, half, j]
        return remote(where, where, c_send.at[s, half, j], c_recv.at[s, half, j], sub=1 - c)

    def from_core(s, half, j):
        where = rows.at[s, 1 - c, half, j]
        return remote(where, where, c_send.at[s, half, j], c_recv.at[s, half, j], sub=1 - c)

    def weight_piece(d, n):
        t = lax.rem(z + d, shards)
        src = (wq, wk, wv)[n].at[y, :, pl.ds(pl.multiple_of(t * widths[n], widths[n]), widths[n])]
        return remote(
            src, weights.at[z, y, :, pl.ds(starts[n], widths[n])],
            w_send.at[d, n], w_recv.at[d, n], seq=t,
        )

    def weight_arrival(d, n):
        s = lax.rem(z + shards - d, shards)
        where = weights.at[s, y, :, pl.ds(starts[n], widths[n])]
        return remote(where, where, w_send.at[d, n], w_recv.at[d, n], seq=s)

    def weight_across(d, half):
        s = lax.rem(z + shards - d, shards)
        where = weights.at[s, half]
        return remote(where, where, y_send.at[d], y_recv.at[d], groups=1 - y)

    def own_weight(n):
        src = (wq, wk, wv)[n].at[:, :, pl.ds(pl.multiple_of(z * widths[n], widths[n]), widths[n])]
        return pltpu.make_async_copy(
            src, weights.at[z, :, :, pl.ds(starts[n], widths[n])], ownw_sem.at[n]
        )

    def sums():
        return remote(mine, theirs, s_send, s_recv, sub=1 - c)

    def add_up(i, _):
        half, j = i // chunks, i % chunks
        values = hidden[half, j].astype(jnp.float32)
        total = jnp.sum(values * values, axis=1, keepdims=True)
        mine[half, j] = jnp.broadcast_to(total, (chunk, HEAD_DIM))
        return 0

    lax.fori_loop(0, 2 * chunks, add_up, 0)
    sums().start()
    sums().wait_recv()

    def normalise(i, _):
        half, j = (x + i // chunks) % 2, i % chunks
        mean = (mine[half, j][:, :1] + theirs[half, j][:, :1]) / (2 * width)
        values = hidden[half, j].astype(jnp.float32) * lax.rsqrt(mean + EPSILON)
        rows[z, c, half, j] = (values * norm_gain[pl.ds(c, 1), :]).astype(jnp.bfloat16)
        for right in (True, False):

            @pl.when((i < chunks) & (z + 1 < shards if right else z > 0))
            def _():
                along(0, j, right).start()

        to_core(z, half, j).start()
        return 0

    lax.fori_loop(0, 2 * chunks, normalise, 0)
    for d in range(1, shards):
        for n in range(3):
            weight_piece(d, n).start()
    for n in range(3):
        own_weight(n).start()

    def has(step, right):
        return z - step >= 0 if right else z + step < shards

    def second_hop(step, j):
        for right in (True, False):

            @pl.when(has(step, right))
            def _():
                s = z - step if right else z + step
                across(s, j, 1 - x).wait_recv()
                to_core(s, 1 - x, j).start()

    def handle(step, j):
        for right in (True, False):

            @pl.when(has(step, right))
            def _():
                s = z - step if right else z + step
                along_recv(step, j, right).wait_recv()

                @pl.when(z + 1 < shards if right else z > 0)
                def _():
                    along(step, j, right).start()

                across(s, j, x).start()
                to_core(s, x, j).start()

    def swap_weights(d):
        for n in range(3):
            weight_arrival(d, n).wait_recv()
        weight_across(d, y).start()

    def turned(u, gain, cosine, sine, factor):
        n = u * lax.rsqrt(jnp.mean(u * u, axis=1, keepdims=True) + EPSILON) * gain
        swapped = pltpu.roll(n, HEAD_DIM // 2, 1)
        return ((n * cosine + swapped * sine) * factor).astype(jnp.bfloat16)

    def project(i):
        m, half = i // 2, i % 2
        s = ((z // 2 + m // 2) % 2) * 2 + (z % 2 + m % 2) % 2
        for j in range(chunks):
            from_core(s, half, j).wait_recv()
        acc = jnp.zeros((2 * BLOCK, 4 * HEAD_DIM), jnp.float32)
        for part in range(2):
            left = rows[s, part, half].reshape(2 * BLOCK, width)
            right = weights[part * shards // 2 : (part + 1) * shards // 2]
            acc = acc + jnp.dot(
                left, right.reshape(width, 4 * HEAD_DIM), preferred_element_type=jnp.float32
            )
        for block in range(2):
            slot = s * 4 + half * 2 + block
            bc, bs = block_turn[0, pl.ds(slot, 1), :], block_turn[1, pl.ds(slot, 1), :]
            wc, ws = within_turn[0], within_turn[1]
            lane = lax.broadcasted_iota(jnp.int32, (BLOCK, HEAD_DIM), 1)
            cosine = bc * wc - bs * ws
            sine = jnp.where(lane < HEAD_DIM // 2, -1.0, 1.0) * (bs * wc + bc * ws)
            at = pl.ds(pl.multiple_of(slot * BLOCK, BLOCK), BLOCK)
            own = acc[block * BLOCK : (block + 1) * BLOCK]
            for h in range(3):
                cols = slice(h * HEAD_DIM, (h + 1) * HEAD_DIM)
                gain, factor = (gains[0:1], QUERY_SCALE) if h < 2 else (gains[1:2], 1.0)
                out[at, cols] = turned(own[:, cols], gain, cosine, sine, factor)
            out[at, 3 * HEAD_DIM :] = own[:, 3 * HEAD_DIM :].astype(jnp.bfloat16)

    for j in range(chunks):
        handle(1, j)
        if j > 0:
            second_hop(1, j - 1)
    swap_weights(1)

    for n in range(2 * chunks + 2):
        if n < 2 * chunks:
            handle(2 + n // chunks, n % chunks)
        if n < 2:
            swap_weights(2 + n)
        if n == 0:
            second_hop(1, chunks - 1)
        elif n <= 2 * chunks:
            second_hop(2 + (n - 1) // chunks, (n - 1) % chunks)
        if n == 2:
            for d in range(1, shards):
                weight_across(d, 1 - y).wait_recv()
            for k in range(3):
                own_weight(k).wait()
        if n >= 2:
            project(n - 2)

    sums().wait_send()
    for d in range(1, shards):
        for n in range(3):
            weight_piece(d, n).wait_send()
        weight_across(d, y).wait_send()
    for step in range(shards):
        for right in (True, False):

            @pl.when(has(step, right) & (z + 1 < shards if right else z > 0))
            def _():
                for j in range(chunks):
                    along(step, j, right).wait_send()

            if step > 0:

                @pl.when(has(step, right))
                def _():
                    s = z - step if right else z + step
                    for j in range(chunks):
                        across(s, j, x).wait_send()
    for s in range(shards):
        for half in range(2):
            for j in range(chunks):
                to_core(s, half, j).wait_send()


def gather_all(hidden, norm_gain, gains, block_turn, within_turn, w_query, w_key, w_value, shards):
    row_count, width = hidden.shape
    depth = w_query.shape[0]
    chunk = row_count // (2 * CHUNKS)
    total = (w_query.shape[1] + w_key.shape[1] + w_value.shape[1]) // shards
    halves = [w.reshape(2, depth // 2, w.shape[1]) for w in (w_query, w_key, w_value)]
    dma = pltpu.SemaphoreType.DMA
    line = dma((shards + 1, CHUNKS))
    anywhere = pl.BlockSpec(memory_space=pl.ANY)
    inside = pl.BlockSpec(memory_space=pltpu.VMEM)
    return pl.pallas_call(
        functools.partial(gather_kernel, shards),
        out_shape=jax.ShapeDtypeStruct((row_count * shards, total), jnp.bfloat16),
        in_specs=[inside] * 5 + [anywhere] * 3,
        out_specs=inside,
        scratch_shapes=[
            pltpu.VMEM((shards, 2, 2, CHUNKS, chunk, width), jnp.bfloat16),
            pltpu.VMEM((shards, 2, depth // 2, total), jnp.bfloat16),
            pltpu.VMEM((2, CHUNKS, chunk, HEAD_DIM), jnp.float32),
            pltpu.VMEM((2, CHUNKS, chunk, HEAD_DIM), jnp.float32),
            line, line, line, line, line, line,
            dma((shards, 2, CHUNKS)), dma((shards, 2, CHUNKS)),
            dma((shards, 3)), dma((shards, 3)), dma((shards,)), dma((shards,)),
            dma((3,)), dma, dma,
        ],
        compiler_params=pltpu.CompilerParams(
            collective_id=0, has_side_effects=True, vmem_limit_bytes=VMEM_LIMIT
        ),
        name="gather_all",
    )(
        hidden.reshape(2, CHUNKS, chunk, width), norm_gain.reshape(2, width), gains,
        block_turn, within_turn, *halves,
    )


def attend_kernel(first, source, q_ref, all_ref, out_ref, k_ref, v_ref):
    b = pl.program_id(0)

    @pl.when(b == 0)
    def _():
        for i in range(k_ref.shape[0] // BLOCK):
            at = pl.ds(pl.multiple_of(source[i] * BLOCK, BLOCK), BLOCK)
            k_ref[i * BLOCK : (i + 1) * BLOCK, :] = all_ref[at, 2 * HEAD_DIM : 3 * HEAD_DIM]
            v_ref[i * BLOCK : (i + 1) * BLOCK, :] = all_ref[at, 3 * HEAD_DIM :]

    span = 2 * BLOCK
    query = jnp.concatenate([q_ref[:, :HEAD_DIM], q_ref[:, HEAD_DIM:]], axis=0)
    start = first[b] * BLOCK
    lowest = jnp.maximum(first[b], b - WINDOW // BLOCK)
    token = b * BLOCK + lax.rem(lax.broadcasted_iota(jnp.int32, (span, span), 0), BLOCK)
    lane = lax.broadcasted_iota(jnp.int32, (span, span), 1)
    least = jnp.maximum(start, token - (WINDOW - 1))

    def step(i, carry):
        acc, total = carry
        at = pl.multiple_of(i * span, span)
        keys = k_ref[pl.ds(at, span), :]
        scores = lax.dot_general(
            query, keys, (((1,), (1,)), ((), ())), preferred_element_type=jnp.float32
        )
        other = lane + at
        allowed = (other <= token) & (other >= least)
        weight = jnp.where(allowed, jnp.exp(scores), 0.0)
        total = total + weight[:, :HEAD_DIM] + weight[:, HEAD_DIM:]
        acc = acc + jnp.dot(
            weight.astype(jnp.bfloat16),
            v_ref[pl.ds(at, span), :],
            preferred_element_type=jnp.float32,
        )
        return acc, total

    zero = jnp.zeros((span, HEAD_DIM), jnp.float32)
    acc, total = lax.fori_loop(lowest // 2, b // 2 + 1, step, (zero, zero))
    result = (acc / jnp.sum(total, axis=1, keepdims=True)).astype(jnp.bfloat16)
    out_ref[:, :HEAD_DIM] = result[:BLOCK]
    out_ref[:, HEAD_DIM:] = result[BLOCK:]


def attend_all(packed, first, source):
    tokens = packed.shape[0]
    return pl.pallas_call(
        attend_kernel,
        grid_spec=pltpu.PrefetchScalarGridSpec(
            num_scalar_prefetch=2,
            grid=(tokens // BLOCK,),
            in_specs=[
                pl.BlockSpec((BLOCK, 2 * HEAD_DIM), lambda i, first, source: (source[i], 0)),
                pl.BlockSpec(packed.shape, lambda i, first, source: (0, 0)),
            ],
            out_specs=pl.BlockSpec((BLOCK, 2 * HEAD_DIM), lambda i, first, source: (i, 0)),
            scratch_shapes=[
                pltpu.VMEM((tokens, HEAD_DIM), jnp.bfloat16),
                pltpu.VMEM((tokens, HEAD_DIM), jnp.bfloat16),
            ],
        ),
        out_shape=jax.ShapeDtypeStruct((tokens, 2 * HEAD_DIM), jnp.bfloat16),
        compiler_params=pltpu.CompilerParams(vmem_limit_bytes=VMEM_LIMIT),
        name="attend_all",
    )(first, source, packed, packed)


def scatter_kernel(shards, result, out, send, recv, own_sem):
    z = lax.axis_index("seq")
    rows, width = out.shape[0], result.shape[1]
    barrier = pltpu.get_barrier_semaphore()
    for d in range(1, shards):
        pl.semaphore_signal(
            barrier, inc=1, device_id={"seq": lax.rem(z + d, shards)}, device_id_type=MESH
        )
    pl.semaphore_wait(barrier, shards - 1)

    def columns(s):
        return out.at[:, pl.ds(pl.multiple_of(s * width, width), width)]

    def part(t):
        return result.at[pl.ds(pl.multiple_of(t * rows, rows), rows), :]

    def outgoing(d):
        t = lax.rem(z + d, shards)
        return remote(part(t), columns(z), send.at[d], recv.at[d], seq=t)

    def incoming(d):
        s = lax.rem(z + shards - d, shards)
        return remote(columns(s), columns(s), send.at[d], recv.at[d], seq=s)

    own = pltpu.make_async_copy(part(z), columns(z), own_sem)
    for d in range(1, shards):
        outgoing(d).start()
    own.start()
    for d in range(1, shards):
        incoming(d).wait_recv()
    own.wait()
    for d in range(1, shards):
        outgoing(d).wait_send()


def scatter_all(result, shards):
    tokens, width = result.shape
    dma = pltpu.SemaphoreType.DMA
    anywhere = pl.BlockSpec(memory_space=pl.ANY)
    return pl.pallas_call(
        functools.partial(scatter_kernel, shards),
        out_shape=jax.ShapeDtypeStruct((tokens // shards, width * shards), jnp.bfloat16),
        in_specs=[anywhere],
        out_specs=anywhere,
        scratch_shapes=[dma((shards,)), dma((shards,)), dma],
        compiler_params=pltpu.CompilerParams(collective_id=1, has_side_effects=True),
        name="scatter_all",
    )(result)


def turn_table(positions):
    half_dim = HEAD_DIM // 2
    frequency = ROPE_BASE ** (-(np.arange(half_dim, dtype=np.float64) * 2.0 / HEAD_DIM))
    angles = np.asarray(positions, np.float64)[:, None] * np.tile(frequency, 2)[None, :]
    return np.stack([np.cos(angles), np.sin(angles)]).astype(np.float32)


def by_heads(
    hidden, norm_gain, w_query, w_key, w_value, query_gain, key_gain, block_source, block_doc
):
    shards = lax.axis_size("seq")
    blocks = block_source.shape[0]
    ids = jnp.arange(blocks, dtype=jnp.int32)
    first = jnp.sum((block_doc[None, :] < block_doc[:, None]).astype(jnp.int32), axis=1)
    arrived = block_source[None, :] == ids[:, None]
    offset = jnp.sum(jnp.where(arrived, (ids - first)[None, :], 0), axis=1)
    picked = (offset[:, None] == ids[None, :])[None, :, :, None]
    table = jnp.asarray(turn_table(np.arange(blocks) * BLOCK))
    block_turn = jnp.sum(jnp.where(picked, table[:, None, :, :], 0.0), axis=2)
    packed = gather_all(
        hidden,
        norm_gain,
        jnp.stack([query_gain, key_gain]),
        block_turn,
        jnp.asarray(turn_table(np.arange(BLOCK))),
        w_query,
        w_key,
        w_value,
        shards,
    )
    return scatter_all(attend_all(packed, first, block_source), shards)


def fits(mesh):
    return (
        mesh.shape["groups"] == 2
        and mesh.shape["head"] == 2
        and mesh.shape["sub"] == 2
        and mesh.shape["seq"] == 4
    )


def solution(mesh):
    placed = (
        P(("groups", "seq"), "sub"),
        P(),
        P("seq", ("head", "sub")),
        P("seq", ("head", "sub")),
        P("seq", ("head", "sub")),
        P(),
        P(),
        P("groups"),
        P("groups"),
    )
    return jax.shard_map(
        by_heads if fits(mesh) else body,
        mesh=mesh,
        in_specs=placed,
        out_specs=P(("groups", "seq"), ("head", "sub")),
        check_vma=False,
    )
```
